32 devices in a mesh: groups: 2 (over y), patch: 16 (over z, x, core).
Axes of the slice: x: 2, y: 2, z: 4, core: 2. Of those that a mesh axis runs over, the one named last changes fastest.
Arguments:
- coarse_depth: float32 [32, 128, 128], P(('groups', 'patch')), parts along dimension 0, may hold values from 1 to 3
- coarse_momentum: float32 [2, 32, 128, 128], P(None, ('groups', 'patch')), parts along dimension 1, may hold values from -3 to 3
- coarse_bed: float32 [32, 128, 128], P(('groups', 'patch')), parts along dimension 0, may hold values from -0.1 to 0.1
- fine_depth: float32 [128, 128, 128], P(('groups', 'patch')), parts along dimension 0, may hold values from 1 to 3
- fine_momentum: float32 [2, 128, 128, 128], P(None, ('groups', 'patch')), parts along dimension 1, may hold values from -3 to 3
- fine_bed: float32 [128, 128, 128], P(('groups', 'patch')), parts along dimension 0, may hold values from -0.1 to 0.1
- coarse_neighbors: int32 [32, 4], P(('groups', 'patch')), parts along dimension 0, may hold values from -1 to 15, as said below
- coarse_children: int32 [32, 4], P(('groups', 'patch')), parts along dimension 0, may hold values from 0 to 63, as said below
- coarse_refined: int32 [32, 4], P(('groups', 'patch')), parts along dimension 0, may hold values from 0 to 1
- fine_parent: int32 [128], P(('groups', 'patch')), parts along dimension 0, may hold values from 0 to 15, as said below
- fine_block: int32 [128], P(('groups', 'patch')), parts along dimension 0, may hold values from 0 to 3, as said below
- fine_active: int32 [128], P(('groups', 'patch')), parts along dimension 0, may hold values from 0 to 1, as said below
- fine_neighbors: int32 [128, 4], P(('groups', 'patch')), parts along dimension 0, may hold values from -1 to 63, as said below
- fill_mode: int32 [128, 4], P(('groups', 'patch')), parts along dimension 0, may hold values from 0 to 1
Outputs:
- coarse_depth_out: float32 [32, 128, 128], P(('groups', 'patch')), parts along dimension 0
- coarse_momentum_out: float32 [2, 32, 128, 128], P(None, ('groups', 'patch')), parts along dimension 1
- fine_depth_out: float32 [128, 128, 128], P(('groups', 'patch')), parts along dimension 0
- fine_momentum_out: float32 [2, 128, 128, 128], P(None, ('groups', 'patch')), parts along dimension 1
The draws below stay inside these ranges and needn't reach their ends.
There are 2 independent parts, one for each index of `groups`. The reference program is written for one: setup_inputs(seed, part) draws one part's arguments, and reference() takes and returns one part's arrays. A program takes and returns all parts, laid end to end along the dimension named above; each array names one. Nothing has to cross between parts.
Inputs may be any that keep to these rules, and one draw needn't show every extreme that they name: `coarse_neighbors`: coarse neighbours are symmetric and lie on a grid of 8 patches a row; patch numbers follow the grid row by row, rows alternating in direction, so two neighbours' numbers differ by at most 15. `fine_parent`: each fine slot's parent is held by the slot's device or the next one along the axis (the last device's next is the first). `fine_block`: each pair of parent and block belongs to exactly one slot. `fine_active`: equals coarse_refined of the slot's parent and block. `coarse_children`: each named child slot is held by the coarse patch's device or the one before it along the axis (the first device's one before is the last), and has that parent and block. `fine_neighbors`: A named neighbour is an active sibling of the same parent, held by the slot's device or one beside it, cyclically; symmetric.
All inputs are finite; a program needn't handle non-finite values.
Results may differ from the reference program's by a relative error of at most 0.0003.
Values sent between devices are 32-bit elements; how exact they have to be, the bound alone decides.
A program may use at most 128 MiB of HBM per device.

```python
import jax
import jax.numpy as jnp
import numpy as np
from jax import lax

PATCH = 128
PF = 4
NC = 16
NF = 64
GRIDX = 8
STEPS = 2


def layout(key):
    key_list = jax.random.split(jax.random.fold_in(key, 101), 7)
    grid_rows = NC // GRIDX
    curve_ids = jnp.arange(NC, dtype=jnp.int32)
    snake_row = curve_ids // GRIDX
    snake_col = jnp.where(snake_row % 2 == 0, curve_ids % GRIDX, GRIDX - 1 - curve_ids % GRIDX)
    placement = (snake_row * GRIDX + snake_col).astype(jnp.int32)
    occupant = jnp.zeros((NC,), jnp.int32).at[placement].set(curve_ids)
    column_pos = placement % GRIDX
    row_pos = placement // GRIDX
    open_east = jax.random.randint(key_list[1], (NC,), 0, 4) > 0
    open_north = jax.random.randint(key_list[2], (NC,), 0, 4) > 0
    west_cell = jnp.maximum(placement - 1, 0)
    east_cell = jnp.minimum(placement + 1, NC - 1)
    south_cell = jnp.maximum(placement - GRIDX, 0)
    north_cell = jnp.minimum(placement + GRIDX, NC - 1)
    west_id = jnp.where((column_pos > 0) & open_east[west_cell], occupant[west_cell], -1)
    east_id = jnp.where((column_pos < GRIDX - 1) & open_east[placement], occupant[east_cell], -1)
    south_id = jnp.where((row_pos > 0) & open_north[south_cell], occupant[south_cell], -1)
    north_id = jnp.where((row_pos < grid_rows - 1) & open_north[placement], occupant[north_cell], -1)
    neighbor_table = jnp.stack([west_id, east_id, south_id, north_id], axis=1).astype(jnp.int32)
    curve_shift = jax.random.randint(key_list[3], (), 1, 4)
    holders = NF // PF
    slot_scores = jax.random.randint(key_list[6], (holders, PF), 0, 4096) * PF + jnp.arange(PF, dtype=jnp.int32)[None, :]
    local_perm = jnp.argsort(slot_scores, axis=1).astype(jnp.int32)
    local_inverse = jnp.argsort(local_perm, axis=1).astype(jnp.int32)
    holder_base = (jnp.arange(holders, dtype=jnp.int32) * PF)[:, None]
    virtual_of = (holder_base + local_perm).reshape(-1).astype(jnp.int32)
    physical_of = (holder_base + local_inverse).reshape(-1).astype(jnp.int32)
    position = (virtual_of + curve_shift) % 4
    parent_ids = (virtual_of + curve_shift) // 4 % NC
    scores = jax.random.randint(key_list[5], (NC, 4), 0, 1024) * 4 + jnp.arange(4, dtype=jnp.int32)[None, :]
    block_order = jnp.argsort(scores, axis=1).astype(jnp.int32)
    block_ids = block_order[parent_ids, position]
    four_ids = jnp.arange(4, dtype=jnp.int32)
    forced = (block_order[:, :1] == four_ids[None, :]).astype(jnp.int32)
    refined = jnp.maximum((jax.random.randint(key_list[4], (NC, 4), 0, 5) >= 2).astype(jnp.int32), forced)
    active = refined[parent_ids, block_ids]
    place_of = jnp.zeros((NC, 4), jnp.int32)
    for spot in range(4):
        place_of = place_of + spot * (block_order[:, spot:spot + 1] == four_ids[None, :]).astype(jnp.int32)
    virtual_children = (4 * jnp.arange(NC, dtype=jnp.int32)[:, None] + place_of - curve_shift) % NF
    children = physical_of[virtual_children]
    kids = children[parent_ids]
    col_half = block_ids % 2
    row_half = block_ids // 2
    partner = jnp.clip(jnp.stack([block_ids - 1, block_ids + 1, block_ids - 2, block_ids + 2], axis=1), 0, 3)
    has_side = jnp.stack([col_half == 1, col_half == 0, row_half == 1, row_half == 0], axis=1)
    sibling = jnp.take_along_axis(kids, partner, axis=1)
    usable = has_side & (active[:, None] > 0) & (active[sibling] > 0)
    fine_table = jnp.where(usable, sibling, -1).astype(jnp.int32)
    return (neighbor_table, children.astype(jnp.int32), refined.astype(jnp.int32), parent_ids.astype(jnp.int32), block_ids.astype(jnp.int32), active.astype(jnp.int32), fine_table)


def draw_coarse_neighbors(key, part):
    return layout(key)[0]


def draw_coarse_children(key, part):
    return layout(key)[1]


def draw_coarse_refined(key, part):
    return layout(key)[2]


def draw_fine_parent(key, part):
    return layout(key)[3]


def draw_fine_block(key, part):
    return layout(key)[4]


def draw_fine_active(key, part):
    return layout(key)[5]


def draw_fine_neighbors(key, part):
    return layout(key)[6]


def draw_fill_mode(key, part):
    key = jax.random.fold_in(key, 7)
    return jax.random.randint(key, (NF, 4), 0, 2).astype(jnp.int32)


def block_scale(rng, dims, shards, smallest, high):
    gain = 1.0
    for dim, blocks in shards:
        heights = jax.random.uniform(jax.random.fold_in(jax.random.fold_in(rng, 6), dim), (blocks,), jnp.float32, smallest / len(shards), high / len(shards))
        gain = gain * jnp.repeat(jnp.exp(heights), dims[dim] // blocks).reshape((-1,) + (1,) * (len(dims) - 1 - dim))
    return gain


def centred(key, shape, spread, limit, cuts=(), kind=jnp.bfloat16):
    result = jax.random.normal(key, shape, jnp.float32) * spread
    if len(cuts) > 0:
        result = block_scale(key, shape, cuts, -0.22, 0.18) * result
    return jnp.clip(result, min=-limit, max=limit).astype(kind)


def setup_inputs(seed: int = 0, part: int = 0) -> dict:
    arg_keys = jax.random.split(jax.random.key(seed), 15)
    own_keys = jax.random.split(jax.random.fold_in(arg_keys[14], part), 15)
    return {
        "coarse_depth": jnp.clip(1.0 + 2.0 * jax.random.uniform(own_keys[0], (NC, PATCH, PATCH), jnp.float32) ** block_scale(own_keys[0], (NC, PATCH, PATCH), ((0, 16),), -0.2, 0.2), 1.0, 3.0),
        "coarse_momentum": centred(own_keys[1], (2, NC, PATCH, PATCH), 0.4, 3.0, ((1, 16),), jnp.float32),
        "coarse_bed": jnp.clip(jax.random.uniform(own_keys[2], (NC, PATCH, PATCH), jnp.float32, -0.1, 0.1) * block_scale(own_keys[2], (NC, PATCH, PATCH), ((0, 16),), -0.4, 0.0), -0.1, 0.1),
        "fine_depth": jnp.clip(1.0 + 2.0 * jax.random.uniform(own_keys[3], (NF, PATCH, PATCH), jnp.float32) ** block_scale(own_keys[3], (NF, PATCH, PATCH), ((0, 16),), -0.2, 0.2), 1.0, 3.0),
        "fine_momentum": centred(own_keys[4], (2, NF, PATCH, PATCH), 0.4, 3.0, ((1, 16),), jnp.float32),
        "fine_bed": jnp.clip(jax.random.uniform(own_keys[5], (NF, PATCH, PATCH), jnp.float32, -0.1, 0.1) * block_scale(own_keys[5], (NF, PATCH, PATCH), ((0, 16),), -0.4, 0.0), -0.1, 0.1),
        "coarse_neighbors": draw_coarse_neighbors(jax.random.fold_in(jax.random.fold_in(arg_keys[14], part), 71), part),
        "coarse_children": draw_coarse_children(jax.random.fold_in(jax.random.fold_in(arg_keys[14], part), 71), part),
        "coarse_refined": draw_coarse_refined(jax.random.fold_in(jax.random.fold_in(arg_keys[14], part), 71), part),
        "fine_parent": draw_fine_parent(jax.random.fold_in(jax.random.fold_in(arg_keys[14], part), 71), part),
        "fine_block": draw_fine_block(jax.random.fold_in(jax.random.fold_in(arg_keys[14], part), 71), part),
        "fine_active": draw_fine_active(jax.random.fold_in(jax.random.fold_in(arg_keys[14], part), 71), part),
        "fine_neighbors": draw_fine_neighbors(jax.random.fold_in(jax.random.fold_in(arg_keys[14], part), 71), part),
        "fill_mode": draw_fill_mode(jax.random.fold_in(jax.random.fold_in(arg_keys[14], part), 71), part),
    }


GRAVITY = 9.81
CFL_NUMBER = 0.3
WALL_SIGN = np.array([[1.0, -1.0, 1.0, 1.0], [1.0, -1.0, 1.0, 1.0], [1.0, 1.0, -1.0, 1.0], [1.0, 1.0, -1.0, 1.0]], np.float32)
SUB_OFFSETS = np.array([-0.375, -0.125, 0.125, 0.375], np.float32)

def rusanov(depth_left, normal_left, along_left, depth_right, normal_right, along_right):
    speed_left = normal_left / depth_left
    speed_right = normal_right / depth_right
    wave_speed = jnp.maximum(jnp.abs(speed_left) + jnp.sqrt(GRAVITY * depth_left), jnp.abs(speed_right) + jnp.sqrt(GRAVITY * depth_right))
    flux_depth = 0.5 * (normal_left + normal_right) - 0.5 * wave_speed * (depth_right - depth_left)
    flux_normal = 0.5 * (normal_left * speed_left + normal_right * speed_right + 0.5 * GRAVITY * (depth_left * depth_left + depth_right * depth_right)) - 0.5 * wave_speed * (normal_right - normal_left)
    flux_along = 0.5 * (along_left * speed_left + along_right * speed_right) - 0.5 * wave_speed * (along_right - along_left)
    return (flux_depth, flux_normal, flux_along)

def advance(padded, step_ratio):
    row_depth = padded[0, :, 1:-1, :]
    row_east = padded[1, :, 1:-1, :]
    row_north = padded[2, :, 1:-1, :]
    xflux_depth, xflux_east, xflux_north = rusanov(row_depth[:, :, :-1], row_east[:, :, :-1], row_north[:, :, :-1], row_depth[:, :, 1:], row_east[:, :, 1:], row_north[:, :, 1:])
    col_depth = padded[0, :, :, 1:-1]
    col_east = padded[1, :, :, 1:-1]
    col_north = padded[2, :, :, 1:-1]
    yflux_depth, yflux_north, yflux_east = rusanov(col_depth[:, :-1], col_north[:, :-1], col_east[:, :-1], col_depth[:, 1:], col_north[:, 1:], col_east[:, 1:])
    centre = padded[:, :, 1:-1, 1:-1]
    bed_level = padded[3]
    slope_east = 0.5 * (bed_level[:, 1:-1, 2:] - bed_level[:, 1:-1, :-2])
    slope_north = 0.5 * (bed_level[:, 2:, 1:-1] - bed_level[:, :-2, 1:-1])
    new_depth = centre[0] - step_ratio * (xflux_depth[:, :, 1:] - xflux_depth[:, :, :-1] + yflux_depth[:, 1:] - yflux_depth[:, :-1])
    new_east = centre[1] - step_ratio * (xflux_east[:, :, 1:] - xflux_east[:, :, :-1] + yflux_east[:, 1:] - yflux_east[:, :-1] + GRAVITY * centre[0] * slope_east)
    new_north = centre[2] - step_ratio * (xflux_north[:, :, 1:] - xflux_north[:, :, :-1] + yflux_north[:, 1:] - yflux_north[:, :-1] + GRAVITY * centre[0] * slope_north)
    return jnp.stack([new_depth, new_east, new_north, centre[3]])

def with_ghosts(state, ghosts):
    west_side = jnp.transpose(ghosts[:, 0], (1, 0, 2))
    east_side = jnp.transpose(ghosts[:, 1], (1, 0, 2))
    south_side = jnp.transpose(ghosts[:, 2], (1, 0, 2))
    north_side = jnp.transpose(ghosts[:, 3], (1, 0, 2))
    middle = jnp.concatenate([west_side[..., None], state, east_side[..., None]], axis=3)
    corner = jnp.zeros_like(west_side[..., :1])
    bottom = jnp.concatenate([corner, south_side, corner], axis=2)[:, :, None, :]
    summit = jnp.concatenate([corner, north_side, corner], axis=2)[:, :, None, :]
    return jnp.concatenate([bottom, middle, summit], axis=2)

def edge_strips(state):
    sides = jnp.stack([state[:, :, :, 0], state[:, :, :, -1], state[:, :, 0, :], state[:, :, -1, :]])
    return jnp.transpose(sides, (2, 0, 1, 3))

def opposite_strips(table, index):
    found = jnp.take(table, index, axis=0)
    return jnp.stack([found[:, 0, 1], found[:, 1, 0], found[:, 2, 3], found[:, 3, 2]], axis=1)

def cycle_lines(state, quarter):
    line_pos = [quarter - 1, 2 * quarter - 1, 2 * quarter, 3 * quarter]
    columns = [state[:, :, :, place] for place in line_pos]
    rowlines = [state[:, :, place, :] for place in line_pos]
    return jnp.transpose(jnp.stack(columns + rowlines), (2, 1, 0, 3))

def coarse_fill(face_lines, block_ids, mode_ids, quarter):
    col_block = 1 + block_ids % 2
    row_block = 1 + block_ids // 2
    line_index = jnp.stack([col_block - 1, col_block + 1, 3 + row_block, 5 + row_block], axis=1)
    start_cell = quarter * jnp.stack([row_block, row_block, col_block, col_block], axis=1)
    pick_table = (line_index[:, :, None] == jnp.arange(8)[None, None, :]).astype(jnp.float32)
    chosen = jnp.einsum('psl,pcln->pscn', pick_table, face_lines, precision=lax.Precision.HIGHEST)
    positions = start_cell[:, :, None] - 1 + jnp.arange(quarter + 2)[None, None, :]
    positions = jnp.broadcast_to(positions[:, :, None, :], chosen.shape[:3] + (quarter + 2,)).astype(jnp.int32)
    window = jnp.take_along_axis(chosen, positions, axis=3)
    middle_val = window[..., 1:-1]
    rising = window[..., 2:] - middle_val
    falling = middle_val - window[..., :-2]
    slope_val = jnp.where(rising * falling > 0, jnp.sign(rising) * jnp.minimum(jnp.abs(rising), jnp.abs(falling)), 0.0)
    weight_mode = mode_ids.astype(jnp.float32)[:, :, None, None]
    return jnp.repeat(middle_val, 4, axis=3) + weight_mode * jnp.repeat(slope_val, 4, axis=3) * jnp.tile(jnp.asarray(SUB_OFFSETS), quarter)

def top_speed(state, live):
    depth_now = state[0]
    fastest = jnp.maximum(jnp.abs(state[1] / depth_now), jnp.abs(state[2] / depth_now)) + jnp.sqrt(GRAVITY * depth_now)
    return jnp.max(fastest * live[:, None, None])

def restrict_blocks(state, quarter):
    part_state = state[:3]
    patch_count = state.shape[1]
    blocks = part_state.reshape(3, patch_count, quarter, 4, quarter, 4).mean(axis=(3, 5))
    return jnp.transpose(blocks, (1, 0, 2, 3))

def insert_blocks(coarse, blocks, refined, quarter):
    for block_id in range(4):
        row_start = quarter * (1 + block_id // 2)
        col_start = quarter * (1 + block_id % 2)
        region = coarse[:3, :, row_start:row_start + quarter, col_start:col_start + quarter]
        fresh = jnp.transpose(blocks[:, block_id], (1, 0, 2, 3))
        merged = jnp.where(refined[:, block_id][None, :, None, None] > 0, fresh, region)
        coarse = coarse.at[:3, :, row_start:row_start + quarter, col_start:col_start + quarter].set(merged)
    return coarse

def reference(coarse_depth, coarse_momentum, coarse_bed, fine_depth, fine_momentum, fine_bed, coarse_neighbors, coarse_children, coarse_refined, fine_parent, fine_block, fine_active, fine_neighbors, fill_mode):
    quarter = coarse_depth.shape[-1] // 4
    coarse = jnp.concatenate([coarse_depth[None], coarse_momentum, coarse_bed[None]])
    fine = jnp.concatenate([fine_depth[None], fine_momentum, fine_bed[None]])
    live = fine_active.astype(jnp.float32)
    every_coarse = jnp.ones((coarse.shape[1],), jnp.float32)
    coarse_valid = (coarse_neighbors >= 0)[:, :, None, None]
    fine_valid = (fine_neighbors >= 0)[:, :, None, None]
    for coarse_step in range(STEPS):
        fastest_all = jnp.maximum(top_speed(coarse, every_coarse), top_speed(fine, live))
        step_ratio = CFL_NUMBER / fastest_all
        strips = edge_strips(coarse)
        wall_ghosts = strips * jnp.asarray(WALL_SIGN)[None, :, :, None]
        ghosts = jnp.where(coarse_valid, opposite_strips(strips, jnp.maximum(coarse_neighbors, 0)), wall_ghosts)
        advanced = advance(with_ghosts(coarse, ghosts), step_ratio)
        old_lines = jnp.take(cycle_lines(coarse, quarter), fine_parent, axis=0)
        new_lines = jnp.take(cycle_lines(advanced, quarter), fine_parent, axis=0)
        for substep in range(4):
            weight_new = substep / 4.0
            face_lines = (1.0 - weight_new) * old_lines + weight_new * new_lines
            from_coarse = coarse_fill(face_lines, fine_block, fill_mode, quarter)
            fine_strips = edge_strips(fine)
            ghosts_fine = jnp.where(fine_valid, opposite_strips(fine_strips, jnp.maximum(fine_neighbors, 0)), from_coarse)
            stepped = advance(with_ghosts(fine, ghosts_fine), step_ratio)
            fine = jnp.where(live[None, :, None, None] > 0, stepped, fine)
        blocks = jnp.take(restrict_blocks(fine, quarter), coarse_children, axis=0)
        coarse = insert_blocks(advanced, blocks, coarse_refined, quarter)
    return (coarse[0], coarse[1:3], fine[0], fine[1:3])
```

```python
import functools

import jax
import jax.numpy as jnp
from jax import lax
from jax.experimental import pallas as pl
from jax.experimental.pallas import tpu as pltpu
from jax.sharding import PartitionSpec as P

STEPS = 2
GRAVITY = 9.81
CFL_NUMBER = 0.3
GRID = 8
SIZE = 128
Q = SIZE // 4
STRIP = 32
COARSE = 4


def nt(a, b):
    return lax.dot_general(
        a, b, (((1,), (1,)), ((), ())), precision=lax.Precision.HIGHEST,
        preferred_element_type=jnp.float32,
    )


def derived(h, m, n):
    r = 1.0 / h
    u = m * r
    v = n * r
    c = jnp.sqrt(GRAVITY * h)
    p = (0.5 * GRAVITY) * (h * h)
    return (h, m, n, jnp.abs(u) + c, jnp.abs(v) + c, m * u + p, n * v + p, m * v)


def flux(left, right):
    a = jnp.maximum(left[3], right[3])
    return (
        (left[1] + right[1]) - a * (right[0] - left[0]),
        (left[4] + right[4]) - a * (right[1] - left[1]),
        (left[5] + right[5]) - a * (right[2] - left[2]),
    )


def along_x(d):
    return (d[0], d[1], d[2], d[3], d[5], d[7])


def along_y(d):
    return (d[0], d[2], d[1], d[4], d[6], d[7])


def speed_tile(h, m, n):
    s = jnp.maximum(jnp.abs(m), jnp.abs(n)) / h + jnp.sqrt(GRAVITY * h)
    return jnp.max(s.reshape(SIZE // 8, 8, SIZE), axis=0)


def kernel(
    devices,
    cd, cm, cb, fd, fm, fb, meta,
    cd_out, cm_out, fd_out, fm_out,
    prev_d, prev_m, prev_b, prev_meta, meta_s, side_s,
    state, bed, slope_x, slope_y, strips, strips_in, top, top_in, lines, wide, gcol, grow, back,
    local_sem, slot_send, slot_recv, edge_send, edge_recv, top_send, top_recv, back_send, back_recv,
):
    me = lax.axis_index("patch")
    nxt = lax.rem(me + 1, devices)
    before = lax.rem(me + devices - 1, devices)
    column = lax.rem(me, GRID)
    upper = lax.rem(me + (2 * GRID - 1) - 2 * column, devices)
    lower = lax.rem(me + devices - 1 - 2 * column, devices)
    partners = [before, nxt, upper, lower]
    opposite_slot = [1, 0, 3, 2]

    barrier = pltpu.get_barrier_semaphore()

    def greet(off, _):
        pl.semaphore_signal(
            barrier, inc=1, device_id={"patch": lax.rem(me + off, devices)},
            device_id_type=pl.DeviceIdType.MESH,
        )
        return 0

    lax.fori_loop(1, devices, greet, 0)

    lane = lax.broadcasted_iota(jnp.int32, (STRIP, SIZE), 1)
    row = lax.broadcasted_iota(jnp.int32, (STRIP, SIZE), 0)
    first_lane, last_lane = lane == 0, lane == SIZE - 1
    first_row, last_row = row == 0, row == STRIP - 1

    own_meta = pltpu.make_async_copy(meta, meta_s.at[1], local_sem.at[0])
    own_meta.start()

    er = lax.broadcasted_iota(jnp.int32, (8, SIZE), 0)
    ec = lax.broadcasted_iota(jnp.int32, (8, SIZE), 1)
    want = jnp.where(er == 0, 2 * Q, jnp.where(er == 1, Q - 1, jnp.where(er == 2, 3 * Q, jnp.where(
        er == 3, 2 * Q - 1, jnp.where(er == 4, 0, SIZE - 1)))))
    pick = (ec == want).astype(jnp.float32)
    ii = lax.broadcasted_iota(jnp.int32, (SIZE, SIZE), 0)
    jj = lax.broadcasted_iota(jnp.int32, (SIZE, SIZE), 1)
    eye = (ii == jj).astype(jnp.float32)
    offset = (lax.rem(ii, 4).astype(jnp.float32) - 1.5) * 0.25
    spread = [(jj == Q * (1 + r) + ii // 4).astype(jnp.float32) for r in range(2)]
    tilt = [s * offset for s in spread]
    gather_columns = [(ii == Q * (1 + r) + jj // 4).astype(jnp.float32) for r in range(2)]

    state[0, COARSE, 0] = cd[0]
    state[0, COARSE, 1] = cm[0, 0]
    state[0, COARSE, 2] = cm[1, 0]
    bed[COARSE] = cb[0]

    def coarse_field(which, f):
        return bed[COARSE] if f == 3 else state[which, COARSE, f]

    def take_lines(which):
        for f in range(4):
            value = coarse_field(which, f)
            found = nt(pick, value)
            for c in range(2):
                for side in range(2):
                    lines[0, which, pl.ds(c * 8 + f * 2 + side, 1), :] = found[c * 2 + side : c * 2 + side + 1]
            for c, (south, north) in enumerate(((Q - 1, 2 * Q), (2 * Q - 1, 3 * Q))):
                lines[1, which, pl.ds(c * 8 + f * 2, 1), :] = value[south : south + 1]
                lines[1, which, pl.ds(c * 8 + f * 2 + 1, 1), :] = value[north : north + 1]
            if which == 0:
                strips[pl.ds(f, 1), :] = found[4:5]
                strips[pl.ds(4 + f, 1), :] = found[5:6]
                strips[pl.ds(8 + f, 1), :] = value[0:1]
                strips[pl.ds(12 + f, 1), :] = value[SIZE - 1 : SIZE]

    def edge_copy(step, p):
        return pltpu.make_async_remote_copy(
            src_ref=strips,
            dst_ref=strips_in.at[step, opposite_slot[p]],
            send_sem=edge_send.at[step, p],
            recv_sem=edge_recv.at[step, opposite_slot[p]],
            device_id={"patch": partners[p]},
            device_id_type=pl.DeviceIdType.MESH,
        )

    def edge_arrival(step, p):
        return pltpu.make_async_remote_copy(
            src_ref=strips,
            dst_ref=strips_in.at[step, p],
            send_sem=edge_send.at[step, p],
            recv_sem=edge_recv.at[step, p],
            device_id={"patch": partners[p]},
            device_id_type=pl.DeviceIdType.MESH,
        )

    def top_copy(step, off):
        return pltpu.make_async_remote_copy(
            src_ref=top.at[step],
            dst_ref=top_in.at[step, off],
            send_sem=top_send.at[step, off],
            recv_sem=top_recv.at[step, off],
            device_id={"patch": lax.rem(me + off, devices)},
            device_id_type=pl.DeviceIdType.MESH,
        )

    own_meta.wait()
    fastest = speed_tile(cd[0], cm[0, 0], cm[1, 0])
    for j in range(4):
        tile = speed_tile(fd[j], fm[0, j], fm[1, j])
        fastest = jnp.maximum(fastest, jnp.where(meta_s[1, j, 0] > 0, tile, 0.0))
    top[0] = fastest
    take_lines(0)
    pl.semaphore_wait(barrier, devices - 1)

    def start_exchange(step):
        def send(off, _):
            top_copy(step, off).start()
            return 0

        lax.fori_loop(1, devices, send, 0)
        for p in range(4):
            edge_copy(step, p).start()

    start_exchange(0)
    to_next = {"patch": nxt}
    moves = [
        pltpu.make_async_remote_copy(
            src_ref=src, dst_ref=dst, send_sem=slot_send.at[i], recv_sem=slot_recv.at[i],
            device_id=to_next, device_id_type=pl.DeviceIdType.MESH,
        )
        for i, (src, dst) in enumerate(((meta, prev_meta), (fb, prev_b), (fd, prev_d), (fm, prev_m)))
    ]
    for move in moves:
        move.start()

    def ghost_column(old, f, shift):
        return pltpu.roll(old, shift, 1)

    def strip_bed(p, gci, lbase, gri, rbase):
        tile = grow[gri, pl.ds(pl.multiple_of(rbase, 8), 8), :]
        nb = [side_s[0, p * 4 + side] for side in range(4)]
        ok = [side_s[1, p * 4 + side] > 0 for side in range(4)]
        value = bed[p]
        big = lax.broadcasted_iota(jnp.int32, (SIZE, SIZE), 1)
        tall = lax.broadcasted_iota(jnp.int32, (SIZE, SIZE), 0)
        g = pltpu.roll(gcol[gci], lax.rem(2 * SIZE - (lbase + 7), SIZE), 1)
        west = jnp.where(ok[0], pltpu.roll(bed[nb[0]], 1, 1), g)
        east = jnp.where(ok[1], pltpu.roll(bed[nb[1]], SIZE - 1, 1), g)
        south = jnp.where(ok[2], bed[nb[2], SIZE - 1 : SIZE, :], tile[6:7])
        north = jnp.where(ok[3], bed[nb[3], 0:1, :], tile[7:8])
        bw = jnp.where(big == 0, west, pltpu.roll(value, 1, 1))
        be = jnp.where(big == SIZE - 1, east, pltpu.roll(value, SIZE - 1, 1))
        bs = jnp.where(tall == 0, south, pltpu.roll(value, 1, 0))
        bn = jnp.where(tall == SIZE - 1, north, pltpu.roll(value, SIZE - 1, 0))
        slope_x[p] = GRAVITY * (be - bw)
        slope_y[p] = GRAVITY * (bn - bs)

    def advance(p, src, gci, lbase, gri, rbase, half):
        dst = 1 - src
        tile = grow[gri, pl.ds(pl.multiple_of(rbase, 8), 8), :]
        nb = [side_s[0, p * 4 + side] for side in range(4)]
        ok = [side_s[1, p * 4 + side] > 0 for side in range(4)]
        live = side_s[2, p] > 0
        for i in range(SIZE // STRIP):
            r0 = i * STRIP
            rows = slice(r0, r0 + STRIP)
            cell = [state[src, p, f, rows, :] for f in range(3)]
            shared = gcol[gci, rows, :]
            ghost = []
            for f in range(3):
                g = pltpu.roll(shared, lax.rem(2 * SIZE - (lbase + f * 2 + 1), SIZE), 1)
                west = pltpu.roll(state[src, nb[0], f, rows, :], 1, 1)
                east = pltpu.roll(state[src, nb[1], f, rows, :], SIZE - 1, 1)
                ghost.append(
                    jnp.where(lane < SIZE // 2, jnp.where(ok[0], west, g), jnp.where(ok[1], east, g))
                )
            if i == 0:
                low = [
                    jnp.where(ok[2], state[src, nb[2], f, SIZE - 1 : SIZE, :], tile[f * 2 : f * 2 + 1])
                    for f in range(3)
                ]
            else:
                low = [state[src, p, f, r0 - 1 : r0, :] for f in range(3)]
            if i == SIZE // STRIP - 1:
                high = [
                    jnp.where(ok[3], state[src, nb[3], f, 0:1, :], tile[f * 2 + 1 : f * 2 + 2])
                    for f in range(3)
                ]
            else:
                high = [state[src, p, f, r0 + STRIP : r0 + STRIP + 1, :] for f in range(3)]
            here = derived(*cell)
            outside = along_x(derived(*ghost))
            hx = along_x(here)
            left = tuple(
                jnp.where(first_lane, o, pltpu.roll(x, 1, 1)) for o, x in zip(outside, hx)
            )
            fx = flux(left, hx)
            fe = flux(hx, outside)
            dx = [
                jnp.where(last_lane, e, pltpu.roll(w, SIZE - 1, 1)) - w for e, w in zip(fe, fx)
            ]
            hy = along_y(here)
            lowy = along_y(derived(*low))
            highy = along_y(derived(*high))
            below = tuple(
                jnp.where(first_row, o, pltpu.roll(y, 1, 0)) for o, y in zip(lowy, hy)
            )
            fy = flux(below, hy)
            fn = flux(tuple(y[STRIP - 1 : STRIP] for y in hy), highy)
            dy = [
                jnp.where(last_row, e, pltpu.roll(w, STRIP - 1, 0)) - w for e, w in zip(fn, fy)
            ]
            h = cell[0]
            new = (
                h - half * (dx[0] + dy[0]),
                cell[1] - half * (dx[1] + dy[2] + h * slope_x[p, rows, :]),
                cell[2] - half * (dx[2] + dy[1] + h * slope_y[p, rows, :]),
            )
            for f in range(3):
                state[dst, p, f, rows, :] = jnp.where(live, new[f], cell[f])

    for side in range(4):
        side_s[0, COARSE * 4 + side] = 0
        side_s[1, COARSE * 4 + side] = 0
    side_s[2, COARSE] = 1

    for step in range(STEPS):
        for p in range(4):
            edge_arrival(step, p).wait_recv()
        for side in range(4):
            n = meta_s[1, 4, side]
            other = slice(((1, 0, 3, 2)[side]) * 4, ((1, 0, 3, 2)[side]) * 4 + 4)
            found = strips_in[step, 3, other, :]
            for p in range(3):
                found = jnp.where(n == partners[p], strips_in[step, p, other, :], found)
            own = strips[side * 4 : side * 4 + 4, :]
            flip = lax.broadcasted_iota(jnp.int32, (4, SIZE), 0) == (1 if side < 2 else 2)
            values = jnp.where(n >= 0, found, jnp.where(flip, -own, own))
            for f in range(4):
                if side < 2:
                    wide[pl.ds(f * 2 + 1 - side, 1), :] = values[f : f + 1]
                else:
                    grow[2, pl.ds(f * 2 + side - 2, 1), :] = values[f : f + 1]
        gcol[2] = nt(eye, jnp.concatenate([wide[...]] * (SIZE // 8), axis=0))
        if step == 0:
            strip_bed(COARSE, 2, 0, 2, 0)

        def arrive(off, best):
            top_copy(step, off).wait_recv()
            return jnp.maximum(best, top_in[step, off])

        fastest = lax.fori_loop(1, devices, arrive, top[step])
        half = (0.5 * CFL_NUMBER) / jnp.max(fastest, keepdims=True)
        advance(COARSE, 0, 2, 0, 2, 0, half)
        take_lines(1)

        if step == 0:
            for move in moves:
                move.wait_recv()
            prev_copy = pltpu.make_async_copy(prev_meta, meta_s.at[0], local_sem.at[1])
            prev_copy.start()
            prev_copy.wait()
            kids = [meta_s[1, 5, b] for b in range(4)]
            for b in range(4):
                index = jnp.minimum(lax.rem(kids[b] - me * 4 + 4 + 4 * devices, 4 * devices), 7)
                near = index >= 4
                there = jnp.where(near, 0, index)
                here_at = jnp.where(near, index - 4, 0)
                which = near.astype(jnp.int32)
                slot = index - 4 * which
                side_s[2, b] = meta_s[which, slot, 0]
                for side in range(4):
                    n = meta_s[which, slot, 1 + side]
                    spot = jnp.where(n == kids[1], 1, jnp.where(n == kids[2], 2, jnp.where(n == kids[3], 3, 0)))
                    side_s[0, b * 4 + side] = spot
                    side_s[1, b * 4 + side] = jnp.where(n >= 0, 1, 0)
                    side_s[3, b * 4 + side] = meta_s[which, slot, 5 + side]
                state[0, b, 0] = jnp.where(near, fd[here_at], prev_d[there])
                state[0, b, 1] = jnp.where(near, fm[0, here_at], prev_m[0, there])
                state[0, b, 2] = jnp.where(near, fm[1, here_at], prev_m[1, there])
                bed[b] = jnp.where(near, fb[here_at], prev_b[there])

        rows64 = lax.broadcasted_iota(jnp.int32, (64, SIZE), 0)
        odd = lax.rem(rows64, 2) == 1
        second = lax.rem(rows64 // 8, 2) == 1
        for kind in range(2):
            parts = []
            for s in range(4):
                w = s / 4.0
                parts.append((1.0 - w) * lines[kind, 0] + w * lines[kind, 1])
            face = jnp.concatenate(parts, axis=0)
            rising = pltpu.roll(face, SIZE - 1, 1) - face
            falling = face - pltpu.roll(face, 1, 1)
            least = jnp.minimum(jnp.abs(rising), jnp.abs(falling))
            grad = jnp.where(rising * falling > 0, jnp.where(rising > 0, least, -least), 0.0)
            for r in range(2):
                if kind == 0:
                    m = [side_s[3, (2 * r + c) * 4 + side].astype(jnp.float32) for c in range(2) for side in (1, 0)]
                else:
                    m = [side_s[3, (2 * c + r) * 4 + side].astype(jnp.float32) for c in range(2) for side in (2, 3)]
                mode = jnp.where(second, jnp.where(odd, m[3], m[2]), jnp.where(odd, m[1], m[0]))
                leaning = grad * mode
                if kind == 0:
                    gcol[r] = nt(spread[r], jnp.concatenate([face, face], axis=0)) + nt(
                        tilt[r], jnp.concatenate([leaning, leaning], axis=0)
                    )
                else:
                    grow[r] = nt(face, spread[r]) + nt(leaning, tilt[r])
        if step == 0:
            for b in range(4):
                strip_bed(b, b // 2, (b % 2) * 8, b % 2, (b // 2) * 8)

        def substep(t, _):
            s, b = t // 4, lax.rem(t, 4)
            r, c = b // 2, lax.rem(b, 2)
            advance(b, lax.rem(s, 2), r, s * 16 + c * 8, c, s * 16 + r * 8, half)
            return 0

        lax.fori_loop(0, 16, substep, 0)

        if step == STEPS - 1:
            home = pltpu.make_async_remote_copy(
                src_ref=state.at[0, pl.ds(0, 4)], dst_ref=back, send_sem=back_send, recv_sem=back_recv,
                device_id={"patch": before}, device_id_type=pl.DeviceIdType.MESH,
            )
            home.start()

        small_lane = lax.broadcasted_iota(jnp.int32, (Q, SIZE), 1)
        for f in range(3):
            state[0, COARSE, f] = state[1, COARSE, f]
        for b in range(4):
            r, c = b // 2, b % 2
            sums = jnp.concatenate(
                [
                    functools.reduce(
                        jnp.add, [state[0, b, f, pl.ds(k, Q, stride=4), :] for k in range(4)]
                    )
                    for f in range(3)
                ],
                axis=0,
            )
            means = lax.dot_general(
                sums * (1.0 / 16.0), spread[c], (((1,), (0,)), ((), ())),
                precision=lax.Precision.HIGHEST, preferred_element_type=jnp.float32,
            )
            low_lane = Q * (1 + c)
            inside = (small_lane >= low_lane) & (small_lane < low_lane + Q)
            refined = meta_s[1, 6, b] > 0
            for f in range(3):
                held = state[0, COARSE, f, Q * (1 + r) : Q * (2 + r), :]
                fresh = jnp.where(refined, means[f * Q : f * Q + Q], held)
                state[0, COARSE, f, Q * (1 + r) : Q * (2 + r), :] = jnp.where(inside, fresh, held)

        for p in range(4):
            edge_arrival(step, p).wait_send()
        if step < STEPS - 1:
            fastest = speed_tile(state[0, COARSE, 0], state[0, COARSE, 1], state[0, COARSE, 2])
            for b in range(4):
                tile = speed_tile(state[0, b, 0], state[0, b, 1], state[0, b, 2])
                fastest = jnp.maximum(fastest, jnp.where(side_s[2, b] > 0, tile, 0.0))
            top[step + 1] = fastest
            take_lines(0)
            start_exchange(step + 1)

    cd_out[0] = state[0, COARSE, 0]
    cm_out[0, 0] = state[0, COARSE, 1]
    cm_out[1, 0] = state[0, COARSE, 2]
    for move in moves:
        move.wait_send()

    def sent(off, _):
        for step in range(STEPS):
            top_copy(step, off).wait_send()
        return 0

    lax.fori_loop(1, devices, sent, 0)
    home.wait()
    for j in range(4):
        mine = meta_s[1, j, 9] == me
        block = meta_s[1, j, 10]
        fd_out[j] = jnp.where(mine, state[0, block, 0], back[block, 0])
        fm_out[0, j] = jnp.where(mine, state[0, block, 1], back[block, 1])
        fm_out[1, j] = jnp.where(mine, state[0, block, 2], back[block, 2])


def local(
    coarse_depth, coarse_momentum, coarse_bed, fine_depth, fine_momentum, fine_bed,
    coarse_neighbors, coarse_children, coarse_refined, fine_parent, fine_block, fine_active,
    fine_neighbors, fill_mode,
):
    devices = lax.axis_size("patch")
    slots = jnp.concatenate(
        [fine_active[:, None], fine_neighbors, fill_mode, fine_parent[:, None], fine_block[:, None]], axis=1
    )
    family = jnp.concatenate([coarse_neighbors, coarse_children, coarse_refined], axis=0)
    meta = jnp.concatenate(
        [
            jnp.pad(slots, ((0, 0), (0, SIZE - slots.shape[1]))),
            jnp.pad(family, ((0, 1), (0, SIZE - family.shape[1]))),
        ],
        axis=0,
    )
    f32, i32 = jnp.float32, jnp.int32
    vmem = pl.BlockSpec(memory_space=pltpu.VMEM)
    dma = pltpu.SemaphoreType.DMA
    return tuple(
        pl.pallas_call(
            functools.partial(kernel, devices),
            out_shape=(
                jax.ShapeDtypeStruct(coarse_depth.shape, f32),
                jax.ShapeDtypeStruct(coarse_momentum.shape, f32),
                jax.ShapeDtypeStruct(fine_depth.shape, f32),
                jax.ShapeDtypeStruct(fine_momentum.shape, f32),
            ),
            in_specs=[vmem] * 7,
            out_specs=(vmem,) * 4,
            scratch_shapes=[
                pltpu.VMEM((4, SIZE, SIZE), f32),
                pltpu.VMEM((2, 4, SIZE, SIZE), f32),
                pltpu.VMEM((4, SIZE, SIZE), f32),
                pltpu.VMEM((8, SIZE), i32),
                pltpu.SMEM((2, 8, SIZE), i32),
                pltpu.SMEM((4, 20), i32),
                pltpu.VMEM((2, 5, 3, SIZE, SIZE), f32),
                pltpu.VMEM((5, SIZE, SIZE), f32),
                pltpu.VMEM((5, SIZE, SIZE), f32),
                pltpu.VMEM((5, SIZE, SIZE), f32),
                pltpu.VMEM((16, SIZE), f32),
                pltpu.VMEM((STEPS, 4, 16, SIZE), f32),
                pltpu.VMEM((STEPS, 8, SIZE), f32),
                pltpu.VMEM((STEPS, devices, 8, SIZE), f32),
                pltpu.VMEM((2, 2, 16, SIZE), f32),
                pltpu.VMEM((8, SIZE), f32),
                pltpu.VMEM((3, SIZE, SIZE), f32),
                pltpu.VMEM((3, 64, SIZE), f32),
                pltpu.VMEM((4, 3, SIZE, SIZE), f32),
                dma((2,)),
                dma((4,)),
                dma((4,)),
                dma((STEPS, 4)),
                dma((STEPS, 4)),
                dma((STEPS, devices)),
                dma((STEPS, devices)),
                dma(()),
                dma(()),
            ],
            compiler_params=pltpu.CompilerParams(
                collective_id=0, has_side_effects=True, vmem_limit_bytes=40 * 2**20
            ),
        )(coarse_depth, coarse_momentum, coarse_bed, fine_depth, fine_momentum, fine_bed, meta)
    )


def solution(mesh):
    lead = P(("groups", "patch"))
    second = P(None, ("groups", "patch"))
    return jax.shard_map(
        local,
        mesh=mesh,
        in_specs=(lead, second, lead, lead, second, lead) + (lead,) * 8,
        out_specs=(lead, second, lead, second),
        check_vma=False,
    )
```

```python
import functools

import jax
import jax.numpy as jnp
from jax import lax
from jax.experimental import pallas as pl
from jax.experimental.pallas import tpu as pltpu
from jax.sharding import PartitionSpec as P

STEPS = 2
GRAVITY = 9.81
CFL_NUMBER = 0.3
GRID = 8
SIZE = 128
Q = SIZE // 4
STRIP = 32
COARSE = 4


def nt(a, b):
    return lax.dot_general(
        a, b, (((1,), (1,)), ((), ())), precision=lax.Precision.HIGHEST,
        preferred_element_type=jnp.float32,
    )


def derived(h, m, n):
    r = 1.0 / h
    u = m * r
    v = n * r
    c = jnp.sqrt(GRAVITY * h)
    p = (0.5 * GRAVITY) * (h * h)
    return (h, m, n, jnp.abs(u) + c, jnp.abs(v) + c, m * u + p, n * v + p, m * v)


def flux(left, right):
    a = jnp.maximum(left[3], right[3])
    return (
        (left[1] + right[1]) - a * (right[0] - left[0]),
        (left[4] + right[4]) - a * (right[1] - left[1]),
        (left[5] + right[5]) - a * (right[2] - left[2]),
    )


def along_x(d):
    return (d[0], d[1], d[2], d[3], d[5], d[7])


def along_y(d):
    return (d[0], d[2], d[1], d[4], d[6], d[7])


def speed_tile(h, m, n):
    s = jnp.maximum(jnp.abs(m), jnp.abs(n)) / h + jnp.sqrt(GRAVITY * h)
    return jnp.max(s.reshape(SIZE // 8, 8, SIZE), axis=0)


def kernel(
    devices,
    cd_in, cm_in, cb_in, fd_in, fm_in, fb_in,
    around_in, kids_in, refined_in, parent_in, block_in, active_in, beside_in, mode_in,
    cd_out, cm_out, fd_out, fm_out,
    fd, fm, fb, around_s, kids_s, refined_s, parent_s, block_s, active_s, beside_s, mode_s,
    prev_d, prev_m, prev_b, prev_beside, prev_mode, side_s,
    state, bed, slope_x, slope_y, strips, strips_in, top, top_in, lines, wide, gcol, grow, back,
    load_sem, local_sem, slot_send, slot_recv, edge_send, edge_recv, top_send, top_recv, back_send, back_recv,
):
    me = lax.axis_index("patch")
    nxt = lax.rem(me + 1, devices)
    before = lax.rem(me + devices - 1, devices)
    column = lax.rem(me, GRID)
    upper = lax.rem(me + (2 * GRID - 1) - 2 * column, devices)
    lower = lax.rem(me + devices - 1 - 2 * column, devices)
    partners = [before, nxt, upper, lower]
    opposite_slot = [1, 0, 3, 2]

    barrier = pltpu.get_barrier_semaphore()

    def greet(off, _):
        pl.semaphore_signal(
            barrier, inc=1, device_id={"patch": lax.rem(me + off, devices)},
            device_id_type=pl.DeviceIdType.MESH,
        )
        return 0

    lax.fori_loop(1, devices, greet, 0)

    lane = lax.broadcasted_iota(jnp.int32, (STRIP, SIZE), 1)
    row = lax.broadcasted_iota(jnp.int32, (STRIP, SIZE), 0)
    first_lane, last_lane = lane == 0, lane == SIZE - 1
    first_row, last_row = row == 0, row == STRIP - 1

    loads = [
        pltpu.make_async_copy(src, dst, load_sem.at[i])
        for i, (src, dst) in enumerate((
            (active_in, active_s), (fd_in, fd), (fm_in, fm),
            (cd_in.at[0], state.at[0, COARSE, 0]), (cm_in.at[0, 0], state.at[0, COARSE, 1]),
            (cm_in.at[1, 0], state.at[0, COARSE, 2]), (cb_in.at[0], bed.at[COARSE]), (fb_in, fb),
            (around_in, around_s), (kids_in, kids_s), (refined_in, refined_s), (parent_in, parent_s),
            (block_in, block_s), (beside_in, beside_s.at[1]), (mode_in, mode_s.at[1]),
        ))
    ]
    for load in loads:
        load.start()

    er = lax.broadcasted_iota(jnp.int32, (8, SIZE), 0)
    ec = lax.broadcasted_iota(jnp.int32, (8, SIZE), 1)
    want = jnp.where(er == 0, 2 * Q, jnp.where(er == 1, Q - 1, jnp.where(er == 2, 3 * Q, jnp.where(
        er == 3, 2 * Q - 1, jnp.where(er == 4, 0, SIZE - 1)))))
    pick = (ec == want).astype(jnp.float32)
    ii = lax.broadcasted_iota(jnp.int32, (SIZE, SIZE), 0)
    jj = lax.broadcasted_iota(jnp.int32, (SIZE, SIZE), 1)
    eye = (ii == jj).astype(jnp.float32)
    offset = (lax.rem(ii, 4).astype(jnp.float32) - 1.5) * 0.25
    spread = [(jj == Q * (1 + r) + ii // 4).astype(jnp.float32) for r in range(2)]
    tilt = [s * offset for s in spread]
    gather_columns = [(ii == Q * (1 + r) + jj // 4).astype(jnp.float32) for r in range(2)]

    def coarse_field(which, f):
        return bed[COARSE] if f == 3 else state[which, COARSE, f]

    def take_lines(which):
        for f in range(4):
            value = coarse_field(which, f)
            found = nt(pick, value)
            for c in range(2):
                for side in range(2):
                    lines[0, which, pl.ds(c * 8 + f * 2 + side, 1), :] = found[c * 2 + side : c * 2 + side + 1]
            for c, (south, north) in enumerate(((Q - 1, 2 * Q), (2 * Q - 1, 3 * Q))):
                lines[1, which, pl.ds(c * 8 + f * 2, 1), :] = value[south : south + 1]
                lines[1, which, pl.ds(c * 8 + f * 2 + 1, 1), :] = value[north : north + 1]
            if which == 0:
                strips[pl.ds(f, 1), :] = found[4:5]
                strips[pl.ds(4 + f, 1), :] = found[5:6]
                strips[pl.ds(8 + f, 1), :] = value[0:1]
                strips[pl.ds(12 + f, 1), :] = value[SIZE - 1 : SIZE]

    def edge_copy(step, p):
        return pltpu.make_async_remote_copy(
            src_ref=strips,
            dst_ref=strips_in.at[step, opposite_slot[p]],
            send_sem=edge_send.at[step, p],
            recv_sem=edge_recv.at[step, opposite_slot[p]],
            device_id={"patch": partners[p]},
            device_id_type=pl.DeviceIdType.MESH,
        )

    def edge_arrival(step, p):
        return pltpu.make_async_remote_copy(
            src_ref=strips,
            dst_ref=strips_in.at[step, p],
            send_sem=edge_send.at[step, p],
            recv_sem=edge_recv.at[step, p],
            device_id={"patch": partners[p]},
            device_id_type=pl.DeviceIdType.MESH,
        )

    def top_copy(step, off):
        return pltpu.make_async_remote_copy(
            src_ref=top.at[step],
            dst_ref=top_in.at[step, off],
            send_sem=top_send.at[step, off],
            recv_sem=top_recv.at[step, off],
            device_id={"patch": lax.rem(me + off, devices)},
            device_id_type=pl.DeviceIdType.MESH,
        )

    for load in loads:
        load.wait()
    fastest = speed_tile(state[0, COARSE, 0], state[0, COARSE, 1], state[0, COARSE, 2])
    for j in range(4):
        tile = speed_tile(fd[j], fm[0, j], fm[1, j])
        fastest = jnp.maximum(fastest, jnp.where(active_s[j] > 0, tile, 0.0))
    top[0] = fastest
    take_lines(0)
    pl.semaphore_wait(barrier, devices - 1)

    def start_exchange(step):
        def send(off, _):
            top_copy(step, off).start()
            return 0

        lax.fori_loop(1, devices, send, 0)
        for p in range(4):
            edge_copy(step, p).start()

    start_exchange(0)
    to_next = {"patch": nxt}
    moves = [
        pltpu.make_async_remote_copy(
            src_ref=src, dst_ref=dst, send_sem=slot_send.at[i], recv_sem=slot_recv.at[i],
            device_id=to_next, device_id_type=pl.DeviceIdType.MESH,
        )
        for i, (src, dst) in enumerate((
            (beside_in, prev_beside), (mode_in, prev_mode), (fb, prev_b), (fd, prev_d), (fm, prev_m)
        ))
    ]
    for move in moves:
        move.start()

    def ghost_column(old, f, shift):
        return pltpu.roll(old, shift, 1)

    def strip_bed(p, gci, lbase, gri, rbase):
        tile = grow[gri, pl.ds(pl.multiple_of(rbase, 8), 8), :]
        nb = [side_s[0, p * 4 + side] for side in range(4)]
        ok = [side_s[1, p * 4 + side] > 0 for side in range(4)]
        value = bed[p]
        big = lax.broadcasted_iota(jnp.int32, (SIZE, SIZE), 1)
        tall = lax.broadcasted_iota(jnp.int32, (SIZE, SIZE), 0)
        g = pltpu.roll(gcol[gci], lax.rem(2 * SIZE - (lbase + 7), SIZE), 1)
        west = jnp.where(ok[0], pltpu.roll(bed[nb[0]], 1, 1), g)
        east = jnp.where(ok[1], pltpu.roll(bed[nb[1]], SIZE - 1, 1), g)
        south = jnp.where(ok[2], bed[nb[2], SIZE - 1 : SIZE, :], tile[6:7])
        north = jnp.where(ok[3], bed[nb[3], 0:1, :], tile[7:8])
        bw = jnp.where(big == 0, west, pltpu.roll(value, 1, 1))
        be = jnp.where(big == SIZE - 1, east, pltpu.roll(value, SIZE - 1, 1))
        bs = jnp.where(tall == 0, south, pltpu.roll(value, 1, 0))
        bn = jnp.where(tall == SIZE - 1, north, pltpu.roll(value, SIZE - 1, 0))
        slope_x[p] = GRAVITY * (be - bw)
        slope_y[p] = GRAVITY * (bn - bs)

    def advance(p, src, gci, lbase, gri, rbase, half):
        dst = 1 - src
        tile = grow[gri, pl.ds(pl.multiple_of(rbase, 8), 8), :]
        nb = [side_s[0, p * 4 + side] for side in range(4)]
        ok = [side_s[1, p * 4 + side] > 0 for side in range(4)]
        live = side_s[2, p] > 0
        for i in range(SIZE // STRIP):
            r0 = i * STRIP
            rows = slice(r0, r0 + STRIP)
            cell = [state[src, p, f, rows, :] for f in range(3)]
            shared = gcol[gci, rows, :]
            ghost = []
            for f in range(3):
                g = pltpu.roll(shared, lax.rem(2 * SIZE - (lbase + f * 2 + 1), SIZE), 1)
                west = pltpu.roll(state[src, nb[0], f, rows, :], 1, 1)
                east = pltpu.roll(state[src, nb[1], f, rows, :], SIZE - 1, 1)
                ghost.append(
                    jnp.where(lane < SIZE // 2, jnp.where(ok[0], west, g), jnp.where(ok[1], east, g))
                )
            if i == 0:
                low = [
                    jnp.where(ok[2], state[src, nb[2], f, SIZE - 1 : SIZE, :], tile[f * 2 : f * 2 + 1])
                    for f in range(3)
                ]
            else:
                low = [state[src, p, f, r0 - 1 : r0, :] for f in range(3)]
            if i == SIZE // STRIP - 1:
                high = [
                    jnp.where(ok[3], state[src, nb[3], f, 0:1, :], tile[f * 2 + 1 : f * 2 + 2])
                    for f in range(3)
                ]
            else:
                high = [state[src, p, f, r0 + STRIP : r0 + STRIP + 1, :] for f in range(3)]
            here = derived(*cell)
            outside = along_x(derived(*ghost))
            hx = along_x(here)
            left = tuple(
                jnp.where(first_lane, o, pltpu.roll(x, 1, 1)) for o, x in zip(outside, hx)
            )
            fx = flux(left, hx)
            fe = flux(hx, outside)
            dx = [
                jnp.where(last_lane, e, pltpu.roll(w, SIZE - 1, 1)) - w for e, w in zip(fe, fx)
            ]
            hy = along_y(here)
            lowy = along_y(derived(*low))
            highy = along_y(derived(*high))
            below = tuple(
                jnp.where(first_row, o, pltpu.roll(y, 1, 0)) for o, y in zip(lowy, hy)
            )
            fy = flux(below, hy)
            fn = flux(tuple(y[STRIP - 1 : STRIP] for y in hy), highy)
            dy = [
                jnp.where(last_row, e, pltpu.roll(w, STRIP - 1, 0)) - w for e, w in zip(fn, fy)
            ]
            h = cell[0]
            new = (
                h - half * (dx[0] + dy[0]),
                cell[1] - half * (dx[1] + dy[2] + h * slope_x[p, rows, :]),
                cell[2] - half * (dx[2] + dy[1] + h * slope_y[p, rows, :]),
            )
            for f in range(3):
                state[dst, p, f, rows, :] = jnp.where(live, new[f], cell[f])

    for side in range(4):
        side_s[0, COARSE * 4 + side] = 0
        side_s[1, COARSE * 4 + side] = 0
    side_s[2, COARSE] = 1

    for step in range(STEPS):
        for p in range(4):
            edge_arrival(step, p).wait_recv()
        for side in range(4):
            n = around_s[0, side]
            other = slice(((1, 0, 3, 2)[side]) * 4, ((1, 0, 3, 2)[side]) * 4 + 4)
            found = strips_in[step, 3, other, :]
            for p in range(3):
                found = jnp.where(n == partners[p], strips_in[step, p, other, :], found)
            own = strips[side * 4 : side * 4 + 4, :]
            flip = lax.broadcasted_iota(jnp.int32, (4, SIZE), 0) == (1 if side < 2 else 2)
            values = jnp.where(n >= 0, found, jnp.where(flip, -own, own))
            for f in range(4):
                if side < 2:
                    wide[pl.ds(f * 2 + 1 - side, 1), :] = values[f : f + 1]
                else:
                    grow[2, pl.ds(f * 2 + side - 2, 1), :] = values[f : f + 1]
        gcol[2] = nt(eye, jnp.concatenate([wide[...]] * (SIZE // 8), axis=0))
        if step == 0:
            strip_bed(COARSE, 2, 0, 2, 0)

        def arrive(off, best):
            top_copy(step, off).wait_recv()
            return jnp.maximum(best, top_in[step, off])

        fastest = lax.fori_loop(1, devices, arrive, top[step])
        half = (0.5 * CFL_NUMBER) / jnp.max(fastest, keepdims=True)
        advance(COARSE, 0, 2, 0, 2, 0, half)
        take_lines(1)

        if step == 0:
            for move in moves:
                move.wait_recv()
            ints = [
                pltpu.make_async_copy(prev_beside, beside_s.at[0], local_sem.at[0]),
                pltpu.make_async_copy(prev_mode, mode_s.at[0], local_sem.at[1]),
            ]
            for copy in ints:
                copy.start()
            for copy in ints:
                copy.wait()
            kids = [kids_s[0, b] for b in range(4)]
            for b in range(4):
                index = jnp.minimum(lax.rem(kids[b] - me * 4 + 4 + 4 * devices, 4 * devices), 7)
                near = index >= 4
                there = jnp.where(near, 0, index)
                here_at = jnp.where(near, index - 4, 0)
                which = near.astype(jnp.int32)
                slot = index - 4 * which
                side_s[2, b] = refined_s[0, b]
                for side in range(4):
                    n = beside_s[which, slot, side]
                    spot = jnp.where(n == kids[1], 1, jnp.where(n == kids[2], 2, jnp.where(n == kids[3], 3, 0)))
                    side_s[0, b * 4 + side] = spot
                    side_s[1, b * 4 + side] = jnp.where(n >= 0, 1, 0)
                    side_s[3, b * 4 + side] = mode_s[which, slot, side]
                state[0, b, 0] = jnp.where(near, fd[here_at], prev_d[there])
                state[0, b, 1] = jnp.where(near, fm[0, here_at], prev_m[0, there])
                state[0, b, 2] = jnp.where(near, fm[1, here_at], prev_m[1, there])
                bed[b] = jnp.where(near, fb[here_at], prev_b[there])

        rows64 = lax.broadcasted_iota(jnp.int32, (64, SIZE), 0)
        odd = lax.rem(rows64, 2) == 1
        second = lax.rem(rows64 // 8, 2) == 1
        for kind in range(2):
            parts = []
            for s in range(4):
                w = s / 4.0
                parts.append((1.0 - w) * lines[kind, 0] + w * lines[kind, 1])
            face = jnp.concatenate(parts, axis=0)
            rising = pltpu.roll(face, SIZE - 1, 1) - face
            falling = face - pltpu.roll(face, 1, 1)
            least = jnp.minimum(jnp.abs(rising), jnp.abs(falling))
            grad = jnp.where(rising * falling > 0, jnp.where(rising > 0, least, -least), 0.0)
            for r in range(2):
                if kind == 0:
                    m = [side_s[3, (2 * r + c) * 4 + side].astype(jnp.float32) for c in range(2) for side in (1, 0)]
                else:
                    m = [side_s[3, (2 * c + r) * 4 + side].astype(jnp.float32) for c in range(2) for side in (2, 3)]
                mode = jnp.where(second, jnp.where(odd, m[3], m[2]), jnp.where(odd, m[1], m[0]))
                leaning = grad * mode
                if kind == 0:
                    gcol[r] = nt(spread[r], jnp.concatenate([face, face], axis=0)) + nt(
                        tilt[r], jnp.concatenate([leaning, leaning], axis=0)
                    )
                else:
                    grow[r] = nt(face, spread[r]) + nt(leaning, tilt[r])
        if step == 0:
            for b in range(4):
                strip_bed(b, b // 2, (b % 2) * 8, b % 2, (b // 2) * 8)

        def substep(t, _):
            s, b = t // 4, lax.rem(t, 4)
            r, c = b // 2, lax.rem(b, 2)
            advance(b, lax.rem(s, 2), r, s * 16 + c * 8, c, s * 16 + r * 8, half)
            return 0

        lax.fori_loop(0, 16, substep, 0)

        if step == STEPS - 1:
            home = pltpu.make_async_remote_copy(
                src_ref=state.at[0, pl.ds(0, 4)], dst_ref=back, send_sem=back_send, recv_sem=back_recv,
                device_id={"patch": before}, device_id_type=pl.DeviceIdType.MESH,
            )
            home.start()

        small_lane = lax.broadcasted_iota(jnp.int32, (Q, SIZE), 1)
        for f in range(3):
            state[0, COARSE, f] = state[1, COARSE, f]
        for b in range(4):
            r, c = b // 2, b % 2
            sums = jnp.concatenate(
                [
                    functools.reduce(
                        jnp.add, [state[0, b, f, pl.ds(k, Q, stride=4), :] for k in range(4)]
                    )
                    for f in range(3)
                ],
                axis=0,
            )
            means = lax.dot_general(
                sums * (1.0 / 16.0), spread[c], (((1,), (0,)), ((), ())),
                precision=lax.Precision.HIGHEST, preferred_element_type=jnp.float32,
            )
            low_lane = Q * (1 + c)
            inside = (small_lane >= low_lane) & (small_lane < low_lane + Q)
            refined = refined_s[0, b] > 0
            for f in range(3):
                held = state[0, COARSE, f, Q * (1 + r) : Q * (2 + r), :]
                fresh = jnp.where(refined, means[f * Q : f * Q + Q], held)
                state[0, COARSE, f, Q * (1 + r) : Q * (2 + r), :] = jnp.where(inside, fresh, held)

        for p in range(4):
            edge_arrival(step, p).wait_send()
        if step < STEPS - 1:
            fastest = speed_tile(state[0, COARSE, 0], state[0, COARSE, 1], state[0, COARSE, 2])
            for b in range(4):
                tile = speed_tile(state[0, b, 0], state[0, b, 1], state[0, b, 2])
                fastest = jnp.maximum(fastest, jnp.where(side_s[2, b] > 0, tile, 0.0))
            top[step + 1] = fastest
            take_lines(0)
            start_exchange(step + 1)

    cd_out[0] = state[0, COARSE, 0]
    cm_out[0, 0] = state[0, COARSE, 1]
    cm_out[1, 0] = state[0, COARSE, 2]
    for move in moves:
        move.wait_send()

    def sent(off, _):
        for step in range(STEPS):
            top_copy(step, off).wait_send()
        return 0

    lax.fori_loop(1, devices, sent, 0)
    home.wait()
    for j in range(4):
        mine = parent_s[j] == me
        block = block_s[j]
        fd_out[j] = jnp.where(mine, state[0, block, 0], back[block, 0])
        fm_out[0, j] = jnp.where(mine, state[0, block, 1], back[block, 1])
        fm_out[1, j] = jnp.where(mine, state[0, block, 2], back[block, 2])


def local(
    coarse_depth, coarse_momentum, coarse_bed, fine_depth, fine_momentum, fine_bed,
    coarse_neighbors, coarse_children, coarse_refined, fine_parent, fine_block, fine_active,
    fine_neighbors, fill_mode,
):
    devices = lax.axis_size("patch")
    f32, i32 = jnp.float32, jnp.int32
    vmem = pl.BlockSpec(memory_space=pltpu.VMEM)
    dma = pltpu.SemaphoreType.DMA
    return tuple(
        pl.pallas_call(
            functools.partial(kernel, devices),
            out_shape=(
                jax.ShapeDtypeStruct(coarse_depth.shape, f32),
                jax.ShapeDtypeStruct(coarse_momentum.shape, f32),
                jax.ShapeDtypeStruct(fine_depth.shape, f32),
                jax.ShapeDtypeStruct(fine_momentum.shape, f32),
            ),
            in_specs=[pl.BlockSpec(memory_space=pl.ANY)] * 14,
            out_specs=(vmem,) * 4,
            scratch_shapes=[
                pltpu.VMEM((4, SIZE, SIZE), f32),
                pltpu.VMEM((2, 4, SIZE, SIZE), f32),
                pltpu.VMEM((4, SIZE, SIZE), f32),
                pltpu.SMEM((1, 4), i32),
                pltpu.SMEM((1, 4), i32),
                pltpu.SMEM((1, 4), i32),
                pltpu.SMEM((4,), i32),
                pltpu.SMEM((4,), i32),
                pltpu.SMEM((4,), i32),
                pltpu.SMEM((2, 4, 4), i32),
                pltpu.SMEM((2, 4, 4), i32),
                pltpu.VMEM((4, SIZE, SIZE), f32),
                pltpu.VMEM((2, 4, SIZE, SIZE), f32),
                pltpu.VMEM((4, SIZE, SIZE), f32),
                pltpu.VMEM((4, 4), i32),
                pltpu.VMEM((4, 4), i32),
                pltpu.SMEM((4, 20), i32),
                pltpu.VMEM((2, 5, 3, SIZE, SIZE), f32),
                pltpu.VMEM((5, SIZE, SIZE), f32),
                pltpu.VMEM((5, SIZE, SIZE), f32),
                pltpu.VMEM((5, SIZE, SIZE), f32),
                pltpu.VMEM((16, SIZE), f32),
                pltpu.VMEM((STEPS, 4, 16, SIZE), f32),
                pltpu.VMEM((STEPS, 8, SIZE), f32),
                pltpu.VMEM((STEPS, devices, 8, SIZE), f32),
                pltpu.VMEM((2, 2, 16, SIZE), f32),
                pltpu.VMEM((8, SIZE), f32),
                pltpu.VMEM((3, SIZE, SIZE), f32),
                pltpu.VMEM((3, 64, SIZE), f32),
                pltpu.VMEM((4, 3, SIZE, SIZE), f32),
                dma((15,)),
                dma((2,)),
                dma((5,)),
                dma((5,)),
                dma((STEPS, 4)),
                dma((STEPS, 4)),
                dma((STEPS, devices)),
                dma((STEPS, devices)),
                dma(()),
                dma(()),
            ],
            compiler_params=pltpu.CompilerParams(
                collective_id=0, has_side_effects=True, vmem_limit_bytes=56 * 2**20
            ),
        )(coarse_depth, coarse_momentum, coarse_bed, fine_depth, fine_momentum, fine_bed,
          coarse_neighbors, coarse_children, coarse_refined, fine_parent, fine_block, fine_active,
          fine_neighbors, fill_mode)
    )


def solution(mesh):
    lead = P(("groups", "patch"))
    second = P(None, ("groups", "patch"))
    return jax.shard_map(
        local,
        mesh=mesh,
        in_specs=(lead, second, lead, lead, second, lead) + (lead,) * 8,
        out_specs=(lead, second, lead, second),
        check_vma=False,
    )
```

```python
import functools

import jax
import jax.numpy as jnp
from jax import lax
from jax.experimental import pallas as pl
from jax.experimental.pallas import tpu as pltpu
from jax.sharding import PartitionSpec as P

STEPS = 2
GRAVITY = 9.81
CFL_NUMBER = 0.3
GRID = 8
SIZE = 128
Q = SIZE // 4
STRIP = 128
COARSE = 4


def nt(a, b):
    return lax.dot_general(
        a, b, (((1,), (1,)), ((), ())), precision=lax.Precision.HIGHEST,
        preferred_element_type=jnp.float32,
    )


def derived(h, m, n):
    r = 1.0 / h
    u = m * r
    v = n * r
    c = jnp.sqrt(GRAVITY * h)
    p = (0.5 * GRAVITY) * (h * h)
    return (h, m, n, jnp.abs(u) + c, jnp.abs(v) + c, m * u + p, n * v + p, m * v)


def flux(left, right):
    a = jnp.maximum(left[3], right[3])
    return (
        (left[1] + right[1]) - a * (right[0] - left[0]),
        (left[4] + right[4]) - a * (right[1] - left[1]),
        (left[5] + right[5]) - a * (right[2] - left[2]),
    )


def along_x(d):
    return (d[0], d[1], d[2], d[3], d[5], d[7])


def along_y(d):
    return (d[0], d[2], d[1], d[4], d[6], d[7])


def speed_tile(h, m, n):
    s = jnp.maximum(jnp.abs(m), jnp.abs(n)) / h + jnp.sqrt(GRAVITY * h)
    return jnp.max(s.reshape(SIZE // 8, 8, SIZE), axis=0)


def kernel(
    devices,
    cd_in, cm_in, cb_in, fd_in, fm_in, fb_in,
    around_in, kids_in, refined_in, parent_in, block_in, active_in, beside_in, mode_in,
    cd_out, cm_out, fd_out, fm_out,
    fd, fm, fb, around_s, kids_s, refined_s, parent_s, block_s, active_s, beside_s, mode_s,
    prev_d, prev_m, prev_b, prev_beside, prev_mode, side_s,
    state, bed, slope_x, slope_y, strips, strips_in, top, top_in, lines, wide, gcol, grow, back,
    load_sem, local_sem, slot_send, slot_recv, edge_send, edge_recv, top_send, top_recv, back_send, back_recv,
):
    me = lax.axis_index("patch")
    nxt = lax.rem(me + 1, devices)
    before = lax.rem(me + devices - 1, devices)
    column = lax.rem(me, GRID)
    upper = lax.rem(me + (2 * GRID - 1) - 2 * column, devices)
    lower = lax.rem(me + devices - 1 - 2 * column, devices)
    partners = [before, nxt, upper, lower]
    opposite_slot = [1, 0, 3, 2]

    barrier = pltpu.get_barrier_semaphore()

    def greet(off, _):
        pl.semaphore_signal(
            barrier, inc=1, device_id={"patch": lax.rem(me + off, devices)},
            device_id_type=pl.DeviceIdType.MESH,
        )
        return 0

    lax.fori_loop(1, devices, greet, 0)

    lane = lax.broadcasted_iota(jnp.int32, (STRIP, SIZE), 1)
    row = lax.broadcasted_iota(jnp.int32, (STRIP, SIZE), 0)
    first_lane, last_lane = lane == 0, lane == SIZE - 1
    first_row, last_row = row == 0, row == STRIP - 1

    loads = [
        pltpu.make_async_copy(src, dst, load_sem.at[i])
        for i, (src, dst) in enumerate((
            (active_in, active_s), (fd_in, fd), (fm_in, fm),
            (cd_in.at[0], state.at[0, COARSE, 0]), (cm_in.at[0, 0], state.at[0, COARSE, 1]),
            (cm_in.at[1, 0], state.at[0, COARSE, 2]), (cb_in.at[0], bed.at[COARSE]), (fb_in, fb),
            (around_in, around_s), (kids_in, kids_s), (refined_in, refined_s), (parent_in, parent_s),
            (block_in, block_s), (beside_in, beside_s.at[1]), (mode_in, mode_s.at[1]),
        ))
    ]
    for load in loads:
        load.start()

    er = lax.broadcasted_iota(jnp.int32, (8, SIZE), 0)
    ec = lax.broadcasted_iota(jnp.int32, (8, SIZE), 1)
    want = jnp.where(er == 0, 2 * Q, jnp.where(er == 1, Q - 1, jnp.where(er == 2, 3 * Q, jnp.where(
        er == 3, 2 * Q - 1, jnp.where(er == 4, 0, SIZE - 1)))))
    pick = (ec == want).astype(jnp.float32)
    ii = lax.broadcasted_iota(jnp.int32, (SIZE, SIZE), 0)
    jj = lax.broadcasted_iota(jnp.int32, (SIZE, SIZE), 1)
    eye = (ii == jj).astype(jnp.float32)
    offset = (lax.rem(ii, 4).astype(jnp.float32) - 1.5) * 0.25
    spread = [(jj == Q * (1 + r) + ii // 4).astype(jnp.float32) for r in range(2)]
    tilt = [s * offset for s in spread]
    gather_columns = [(ii == Q * (1 + r) + jj // 4).astype(jnp.float32) for r in range(2)]

    def coarse_field(which, f):
        return bed[COARSE] if f == 3 else state[which, COARSE, f]

    def take_lines(which):
        for f in range(4):
            value = coarse_field(which, f)
            found = nt(pick, value)
            for c in range(2):
                for side in range(2):
                    lines[0, which, pl.ds(c * 8 + f * 2 + side, 1), :] = found[c * 2 + side : c * 2 + side + 1]
            for c, (south, north) in enumerate(((Q - 1, 2 * Q), (2 * Q - 1, 3 * Q))):
                lines[1, which, pl.ds(c * 8 + f * 2, 1), :] = value[south : south + 1]
                lines[1, which, pl.ds(c * 8 + f * 2 + 1, 1), :] = value[north : north + 1]
            if which == 0:
                strips[pl.ds(f, 1), :] = found[4:5]
                strips[pl.ds(4 + f, 1), :] = found[5:6]
                strips[pl.ds(8 + f, 1), :] = value[0:1]
                strips[pl.ds(12 + f, 1), :] = value[SIZE - 1 : SIZE]

    def edge_copy(step, p):
        return pltpu.make_async_remote_copy(
            src_ref=strips,
            dst_ref=strips_in.at[step, opposite_slot[p]],
            send_sem=edge_send.at[step, p],
            recv_sem=edge_recv.at[step, opposite_slot[p]],
            device_id={"patch": partners[p]},
            device_id_type=pl.DeviceIdType.MESH,
        )

    def edge_arrival(step, p):
        return pltpu.make_async_remote_copy(
            src_ref=strips,
            dst_ref=strips_in.at[step, p],
            send_sem=edge_send.at[step, p],
            recv_sem=edge_recv.at[step, p],
            device_id={"patch": partners[p]},
            device_id_type=pl.DeviceIdType.MESH,
        )

    def top_copy(step, off):
        return pltpu.make_async_remote_copy(
            src_ref=top.at[step],
            dst_ref=top_in.at[step, off],
            send_sem=top_send.at[step, off],
            recv_sem=top_recv.at[step, off],
            device_id={"patch": lax.rem(me + off, devices)},
            device_id_type=pl.DeviceIdType.MESH,
        )

    for load in loads:
        load.wait()
    fastest = speed_tile(state[0, COARSE, 0], state[0, COARSE, 1], state[0, COARSE, 2])
    for j in range(4):
        tile = speed_tile(fd[j], fm[0, j], fm[1, j])
        fastest = jnp.maximum(fastest, jnp.where(active_s[j] > 0, tile, 0.0))
    top[0] = fastest
    take_lines(0)
    pl.semaphore_wait(barrier, devices - 1)

    def start_exchange(step):
        def send(off, _):
            top_copy(step, off).start()
            return 0

        lax.fori_loop(1, devices, send, 0)
        for p in range(4):
            edge_copy(step, p).start()

    start_exchange(0)
    to_next = {"patch": nxt}
    moves = [
        pltpu.make_async_remote_copy(
            src_ref=src, dst_ref=dst, send_sem=slot_send.at[i], recv_sem=slot_recv.at[i],
            device_id=to_next, device_id_type=pl.DeviceIdType.MESH,
        )
        for i, (src, dst) in enumerate((
            (beside_in, prev_beside), (mode_in, prev_mode), (fb, prev_b), (fd, prev_d), (fm, prev_m)
        ))
    ]
    for move in moves:
        move.start()

    def ghost_column(old, f, shift):
        return pltpu.roll(old, shift, 1)

    def strip_bed(p, gci, lbase, gri, rbase):
        tile = grow[gri, pl.ds(pl.multiple_of(rbase, 8), 8), :]
        nb = [side_s[0, p * 4 + side] for side in range(4)]
        ok = [side_s[1, p * 4 + side] > 0 for side in range(4)]
        value = bed[p]
        big = lax.broadcasted_iota(jnp.int32, (SIZE, SIZE), 1)
        tall = lax.broadcasted_iota(jnp.int32, (SIZE, SIZE), 0)
        g = pltpu.roll(gcol[gci], lax.rem(2 * SIZE - (lbase + 7), SIZE), 1)
        west = jnp.where(ok[0], pltpu.roll(bed[nb[0]], 1, 1), g)
        east = jnp.where(ok[1], pltpu.roll(bed[nb[1]], SIZE - 1, 1), g)
        south = jnp.where(ok[2], bed[nb[2], SIZE - 1 : SIZE, :], tile[6:7])
        north = jnp.where(ok[3], bed[nb[3], 0:1, :], tile[7:8])
        bw = jnp.where(big == 0, west, pltpu.roll(value, 1, 1))
        be = jnp.where(big == SIZE - 1, east, pltpu.roll(value, SIZE - 1, 1))
        bs = jnp.where(tall == 0, south, pltpu.roll(value, 1, 0))
        bn = jnp.where(tall == SIZE - 1, north, pltpu.roll(value, SIZE - 1, 0))
        slope_x[p] = GRAVITY * (be - bw)
        slope_y[p] = GRAVITY * (bn - bs)

    def advance(p, src, gci, lbase, gri, rbase, half):
        dst = 1 - src
        tile = grow[gri, pl.ds(pl.multiple_of(rbase, 8), 8), :]
        nb = [side_s[0, p * 4 + side] for side in range(4)]
        ok = [side_s[1, p * 4 + side] > 0 for side in range(4)]
        live = side_s[2, p] > 0
        for i in range(SIZE // STRIP):
            r0 = i * STRIP
            rows = slice(r0, r0 + STRIP)
            cell = [state[src, p, f, rows, :] for f in range(3)]
            shared = gcol[gci, rows, :]
            ghost = []
            for f in range(3):
                g = pltpu.roll(shared, lax.rem(2 * SIZE - (lbase + f * 2 + 1), SIZE), 1)
                west = pltpu.roll(state[src, nb[0], f, rows, :], 1, 1)
                east = pltpu.roll(state[src, nb[1], f, rows, :], SIZE - 1, 1)
                ghost.append(
                    jnp.where(lane < SIZE // 2, jnp.where(ok[0], west, g), jnp.where(ok[1], east, g))
                )
            if i == 0:
                low = [
                    jnp.where(ok[2], state[src, nb[2], f, SIZE - 1 : SIZE, :], tile[f * 2 : f * 2 + 1])
                    for f in range(3)
                ]
            else:
                low = [state[src, p, f, r0 - 1 : r0, :] for f in range(3)]
            if i == SIZE // STRIP - 1:
                high = [
                    jnp.where(ok[3], state[src, nb[3], f, 0:1, :], tile[f * 2 + 1 : f * 2 + 2])
                    for f in range(3)
                ]
            else:
                high = [state[src, p, f, r0 + STRIP : r0 + STRIP + 1, :] for f in range(3)]
            here = derived(*cell)
            outside = along_x(derived(*ghost))
            hx = along_x(here)
            left = tuple(
                jnp.where(first_lane, o, pltpu.roll(x, 1, 1)) for o, x in zip(outside, hx)
            )
            fx = flux(left, hx)
            fe = flux(hx, outside)
            dx = [
                jnp.where(last_lane, e, pltpu.roll(w, SIZE - 1, 1)) - w for e, w in zip(fe, fx)
            ]
            hy = along_y(here)
            lowy = along_y(derived(*low))
            highy = along_y(derived(*high))
            below = tuple(
                jnp.where(first_row, o, pltpu.roll(y, 1, 0)) for o, y in zip(lowy, hy)
            )
            fy = flux(below, hy)
            fn = flux(tuple(y[STRIP - 1 : STRIP] for y in hy), highy)
            dy = [
                jnp.where(last_row, e, pltpu.roll(w, STRIP - 1, 0)) - w for e, w in zip(fn, fy)
            ]
            h = cell[0]
            new = (
                h - half * (dx[0] + dy[0]),
                cell[1] - half * (dx[1] + dy[2] + h * slope_x[p, rows, :]),
                cell[2] - half * (dx[2] + dy[1] + h * slope_y[p, rows, :]),
            )
            for f in range(3):
                state[dst, p, f, rows, :] = jnp.where(live, new[f], cell[f])

    def home_copy(b):
        return pltpu.make_async_remote_copy(
            src_ref=state.at[0, b], dst_ref=back.at[b], send_sem=back_send.at[b], recv_sem=back_recv.at[b],
            device_id={"patch": before}, device_id_type=pl.DeviceIdType.MESH,
        )

    for side in range(4):
        side_s[0, COARSE * 4 + side] = 0
        side_s[1, COARSE * 4 + side] = 0
    side_s[2, COARSE] = 1

    for step in range(STEPS):
        for p in range(4):
            edge_arrival(step, p).wait_recv()
        for side in range(4):
            n = around_s[0, side]
            other = slice(((1, 0, 3, 2)[side]) * 4, ((1, 0, 3, 2)[side]) * 4 + 4)
            found = strips_in[step, 3, other, :]
            for p in range(3):
                found = jnp.where(n == partners[p], strips_in[step, p, other, :], found)
            own = strips[side * 4 : side * 4 + 4, :]
            flip = lax.broadcasted_iota(jnp.int32, (4, SIZE), 0) == (1 if side < 2 else 2)
            values = jnp.where(n >= 0, found, jnp.where(flip, -own, own))
            for f in range(4):
                if side < 2:
                    wide[pl.ds(f * 2 + 1 - side, 1), :] = values[f : f + 1]
                else:
                    grow[2, pl.ds(f * 2 + side - 2, 1), :] = values[f : f + 1]
        gcol[2] = nt(eye, jnp.concatenate([wide[...]] * (SIZE // 8), axis=0))
        if step == 0:
            strip_bed(COARSE, 2, 0, 2, 0)

        def arrive(off, best):
            top_copy(step, off).wait_recv()
            return jnp.maximum(best, top_in[step, off])

        fastest = lax.fori_loop(1, devices, arrive, top[step])
        half = (0.5 * CFL_NUMBER) / jnp.max(fastest, keepdims=True)
        advance(COARSE, 0, 2, 0, 2, 0, half)
        take_lines(1)

        if step == 0:
            for move in moves:
                move.wait_recv()
            ints = [
                pltpu.make_async_copy(prev_beside, beside_s.at[0], local_sem.at[0]),
                pltpu.make_async_copy(prev_mode, mode_s.at[0], local_sem.at[1]),
            ]
            for copy in ints:
                copy.start()
            for copy in ints:
                copy.wait()
            kids = [kids_s[0, b] for b in range(4)]
            for b in range(4):
                index = jnp.minimum(lax.rem(kids[b] - me * 4 + 4 + 4 * devices, 4 * devices), 7)
                near = index >= 4
                there = jnp.where(near, 0, index)
                here_at = jnp.where(near, index - 4, 0)
                which = near.astype(jnp.int32)
                slot = index - 4 * which
                side_s[2, b] = refined_s[0, b]
                for side in range(4):
                    n = beside_s[which, slot, side]
                    spot = jnp.where(n == kids[1], 1, jnp.where(n == kids[2], 2, jnp.where(n == kids[3], 3, 0)))
                    side_s[0, b * 4 + side] = spot
                    side_s[1, b * 4 + side] = jnp.where(n >= 0, 1, 0)
                    side_s[3, b * 4 + side] = mode_s[which, slot, side]
                state[0, b, 0] = jnp.where(near, fd[here_at], prev_d[there])
                state[0, b, 1] = jnp.where(near, fm[0, here_at], prev_m[0, there])
                state[0, b, 2] = jnp.where(near, fm[1, here_at], prev_m[1, there])
                bed[b] = jnp.where(near, fb[here_at], prev_b[there])

        rows64 = lax.broadcasted_iota(jnp.int32, (64, SIZE), 0)
        odd = lax.rem(rows64, 2) == 1
        second = lax.rem(rows64 // 8, 2) == 1
        for kind in range(2):
            parts = []
            for s in range(4):
                w = s / 4.0
                parts.append((1.0 - w) * lines[kind, 0] + w * lines[kind, 1])
            face = jnp.concatenate(parts, axis=0)
            rising = pltpu.roll(face, SIZE - 1, 1) - face
            falling = face - pltpu.roll(face, 1, 1)
            least = jnp.minimum(jnp.abs(rising), jnp.abs(falling))
            grad = jnp.where(rising * falling > 0, jnp.where(rising > 0, least, -least), 0.0)
            for r in range(2):
                if kind == 0:
                    m = [side_s[3, (2 * r + c) * 4 + side].astype(jnp.float32) for c in range(2) for side in (1, 0)]
                else:
                    m = [side_s[3, (2 * c + r) * 4 + side].astype(jnp.float32) for c in range(2) for side in (2, 3)]
                mode = jnp.where(second, jnp.where(odd, m[3], m[2]), jnp.where(odd, m[1], m[0]))
                leaning = grad * mode
                if kind == 0:
                    gcol[r] = nt(spread[r], jnp.concatenate([face, face], axis=0)) + nt(
                        tilt[r], jnp.concatenate([leaning, leaning], axis=0)
                    )
                else:
                    grow[r] = nt(face, spread[r]) + nt(leaning, tilt[r])
        if step == 0:
            for b in range(4):
                strip_bed(b, b // 2, (b % 2) * 8, b % 2, (b // 2) * 8)

        def substep(t, _):
            s, b = t // 4, lax.rem(t, 4)
            r, c = b // 2, lax.rem(b, 2)
            advance(b, lax.rem(s, 2), r, s * 16 + c * 8, c, s * 16 + r * 8, half)
            return 0

        if step < STEPS - 1:
            lax.fori_loop(0, 16, substep, 0)
        else:
            lax.fori_loop(0, 12, substep, 0)

            def last(b, _):
                substep(12 + b, 0)
                home_copy(b).start()
                return 0

            lax.fori_loop(0, 4, last, 0)

        small_lane = lax.broadcasted_iota(jnp.int32, (Q, SIZE), 1)
        for f in range(3):
            state[0, COARSE, f] = state[1, COARSE, f]
        for b in range(4):
            r, c = b // 2, b % 2
            sums = jnp.concatenate(
                [
                    functools.reduce(
                        jnp.add, [state[0, b, f, pl.ds(k, Q, stride=4), :] for k in range(4)]
                    )
                    for f in range(3)
                ],
                axis=0,
            )
            means = lax.dot_general(
                sums * (1.0 / 16.0), spread[c], (((1,), (0,)), ((), ())),
                precision=lax.Precision.HIGHEST, preferred_element_type=jnp.float32,
            )
            low_lane = Q * (1 + c)
            inside = (small_lane >= low_lane) & (small_lane < low_lane + Q)
            refined = refined_s[0, b] > 0
            for f in range(3):
                held = state[0, COARSE, f, Q * (1 + r) : Q * (2 + r), :]
                fresh = jnp.where(refined, means[f * Q : f * Q + Q], held)
                state[0, COARSE, f, Q * (1 + r) : Q * (2 + r), :] = jnp.where(inside, fresh, held)

        for p in range(4):
            edge_arrival(step, p).wait_send()
        if step < STEPS - 1:
            fastest = speed_tile(state[0, COARSE, 0], state[0, COARSE, 1], state[0, COARSE, 2])
            for b in range(4):
                tile = speed_tile(state[0, b, 0], state[0, b, 1], state[0, b, 2])
                fastest = jnp.maximum(fastest, jnp.where(side_s[2, b] > 0, tile, 0.0))
            top[step + 1] = fastest
            take_lines(0)
            start_exchange(step + 1)

    cd_out[0] = state[0, COARSE, 0]
    cm_out[0, 0] = state[0, COARSE, 1]
    cm_out[1, 0] = state[0, COARSE, 2]
    for move in moves:
        move.wait_send()

    def sent(off, _):
        for step in range(STEPS):
            top_copy(step, off).wait_send()
        return 0

    lax.fori_loop(1, devices, sent, 0)
    for b in range(4):
        home_copy(b).wait()
    for j in range(4):
        mine = parent_s[j] == me
        block = block_s[j]
        fd_out[j] = jnp.where(mine, state[0, block, 0], back[block, 0])
        fm_out[0, j] = jnp.where(mine, state[0, block, 1], back[block, 1])
        fm_out[1, j] = jnp.where(mine, state[0, block, 2], back[block, 2])


def local(
    coarse_depth, coarse_momentum, coarse_bed, fine_depth, fine_momentum, fine_bed,
    coarse_neighbors, coarse_children, coarse_refined, fine_parent, fine_block, fine_active,
    fine_neighbors, fill_mode,
):
    devices = lax.axis_size("patch")
    f32, i32 = jnp.float32, jnp.int32
    vmem = pl.BlockSpec(memory_space=pltpu.VMEM)
    dma = pltpu.SemaphoreType.DMA
    return tuple(
        pl.pallas_call(
            functools.partial(kernel, devices),
            out_shape=(
                jax.ShapeDtypeStruct(coarse_depth.shape, f32),
                jax.ShapeDtypeStruct(coarse_momentum.shape, f32),
                jax.ShapeDtypeStruct(fine_depth.shape, f32),
                jax.ShapeDtypeStruct(fine_momentum.shape, f32),
            ),
            in_specs=[pl.BlockSpec(memory_space=pl.ANY)] * 14,
            out_specs=(vmem,) * 4,
            scratch_shapes=[
                pltpu.VMEM((4, SIZE, SIZE), f32),
                pltpu.VMEM((2, 4, SIZE, SIZE), f32),
                pltpu.VMEM((4, SIZE, SIZE), f32),
                pltpu.SMEM((1, 4), i32),
                pltpu.SMEM((1, 4), i32),
                pltpu.SMEM((1, 4), i32),
                pltpu.SMEM((4,), i32),
                pltpu.SMEM((4,), i32),
                pltpu.SMEM((4,), i32),
                pltpu.SMEM((2, 4, 4), i32),
                pltpu.SMEM((2, 4, 4), i32),
                pltpu.VMEM((4, SIZE, SIZE), f32),
                pltpu.VMEM((2, 4, SIZE, SIZE), f32),
                pltpu.VMEM((4, SIZE, SIZE), f32),
                pltpu.VMEM((4, 4), i32),
                pltpu.VMEM((4, 4), i32),
                pltpu.SMEM((4, 20), i32),
                pltpu.VMEM((2, 5, 3, SIZE, SIZE), f32),
                pltpu.VMEM((5, SIZE, SIZE), f32),
                pltpu.VMEM((5, SIZE, SIZE), f32),
                pltpu.VMEM((5, SIZE, SIZE), f32),
                pltpu.VMEM((16, SIZE), f32),
                pltpu.VMEM((STEPS, 4, 16, SIZE), f32),
                pltpu.VMEM((STEPS, 8, SIZE), f32),
                pltpu.VMEM((STEPS, devices, 8, SIZE), f32),
                pltpu.VMEM((2, 2, 16, SIZE), f32),
                pltpu.VMEM((8, SIZE), f32),
                pltpu.VMEM((3, SIZE, SIZE), f32),
                pltpu.VMEM((3, 64, SIZE), f32),
                pltpu.VMEM((4, 3, SIZE, SIZE), f32),
                dma((15,)),
                dma((2,)),
                dma((5,)),
                dma((5,)),
                dma((STEPS, 4)),
                dma((STEPS, 4)),
                dma((STEPS, devices)),
                dma((STEPS, devices)),
                dma((4,)),
                dma((4,)),
            ],
            compiler_params=pltpu.CompilerParams(
                collective_id=0, has_side_effects=True, vmem_limit_bytes=56 * 2**20
            ),
        )(coarse_depth, coarse_momentum, coarse_bed, fine_depth, fine_momentum, fine_bed,
          coarse_neighbors, coarse_children, coarse_refined, fine_parent, fine_block, fine_active,
          fine_neighbors, fill_mode)
    )


def solution(mesh):
    lead = P(("groups", "patch"))
    second = P(None, ("groups", "patch"))
    return jax.shard_map(
        local,
        mesh=mesh,
        in_specs=(lead, second, lead, lead, second, lead) + (lead,) * 8,
        out_specs=(lead, second, lead, second),
        check_vma=False,
    )
```
